512 devices in a mesh: section: 32 (over y, x, z_hi), fsdp: 16 (over z_lo, core).
Axes of the slice: x: 4, y: 4, z: 16 (z_hi: 2, z_lo: 8; z = z_hi * 8 + z_lo), core: 2. Of those that a mesh axis runs over, the one named last changes fastest.
Arguments:
- activations: bfloat16 [32, 6144, 2304], P('section', 'fsdp'), may hold values from -6 to 6
- pre_gain: float32 [32, 2304], P('section'), may hold values from 0.5 to 2
- post_gain: float32 [32, 2304], P('section'), may hold values from 0.5 to 2
- w_query: bfloat16 [32, 2304, 1024], P('section', 'fsdp'), may hold values from -2 to 2
- w_keyval: bfloat16 [32, 2304, 1024], P('section', 'fsdp'), may hold values from -0.125 to 0.125
- w_out: bfloat16 [32, 1024, 2304], P('section', 'fsdp'), may hold values from -0.1875 to 0.1875
Outputs:
- advanced: bfloat16 [32, 6144, 2304], P('section', 'fsdp')
The draws below stay inside these ranges and needn't reach their ends.
All inputs are finite; a program needn't handle non-finite values.
Results may differ from the reference program's by a relative error of at most 0.012.
The reference program's roundings to bfloat16 on the way (of `incoming`, `normed`, `probs` and `context`) count: a program that leaves them out, or rounds other values in their place, can miss the bound.
Values may be sent and summed in bfloat16 or wider, within the bound.
No kernel may reach another device: no remote copies, remote signals or barrier semaphores. Data moves between devices by JAX's collectives and lax.ppermute only.
A program may use at most 64 MiB of HBM per device.

```python
import math
import jax
import jax.numpy as jnp
from jax import lax

D = 2304
HEADS = 16
KV_HEADS = 8
HEAD_DIM = 64
SEQ = 384
SECTIONS = 32
ROWS = 6144
QW = 1024
KVW = 512


def draw_w_query(key, part):
    key = jax.random.fold_in(key, 11)
    key_entry, key_rank, key_jitter = jax.random.split(key, 3)
    section_keys = jax.random.split(key_rank, SECTIONS)
    ranks = jax.vmap(lambda single: jax.random.permutation(single, HEADS))(section_keys).astype(jnp.float32)
    jitter = jax.random.uniform(key_jitter, (SECTIONS, HEADS), jnp.float32)
    head_scale = jnp.exp((ranks + jitter) / HEADS * math.log(24.0))
    entries = jax.random.truncated_normal(key_entry, -4.0, 4.0, (SECTIONS, D, HEADS, HEAD_DIM), jnp.float32)
    weights = entries * head_scale[:, None, :, None] * D ** (-0.5)
    return weights.reshape(SECTIONS, D, HEADS * HEAD_DIM).astype(jnp.bfloat16)


def block_levels(key, shape, cuts, least, high):
    def one(axis_at, parts):
        draws = jax.random.uniform(jax.random.fold_in(jax.random.fold_in(key, 6), axis_at), (parts,), jnp.float32, least / len(cuts), high / len(cuts))
        return jnp.repeat(jnp.exp(draws), shape[axis_at] // parts).reshape((-1,) + (1,) * (len(shape) - axis_at - 1))

    level = one(*cuts[0])
    for cut in cuts[1:]:
        level = level * one(*cut)
    return level


def gaussian(key, dims, spread, most, shards=(), kind=jnp.bfloat16):
    level = block_levels(key, dims, shards, -0.22, 0.18) if shards else 1.0
    drawn = jax.random.normal(key, dims, jnp.float32) * spread * level
    return jnp.minimum(jnp.maximum(drawn, -most), most).astype(kind)


def setup_inputs(seed: int = 0) -> dict:
    streams_of = jax.random.split(jax.random.key(seed), 7)
    return {
        "activations": gaussian(streams_of[0], (SECTIONS, ROWS, D), 1.0, 6.0, ((0, 32), (1, 16))),
        "pre_gain": jnp.clip(jnp.exp(math.log(2.0) - 1.3862944 * jax.random.uniform(streams_of[1], (SECTIONS, D), jnp.float32) ** block_levels(streams_of[1], (SECTIONS, D), ((0, 32),), -0.2, 0.2)), 0.5, 2.0),
        "post_gain": jnp.clip(jnp.exp(math.log(2.0) - 1.3862944 * jax.random.uniform(streams_of[2], (SECTIONS, D), jnp.float32) ** block_levels(streams_of[2], (SECTIONS, D), ((0, 32),), -0.2, 0.2)), 0.5, 2.0),
        "w_query": draw_w_query(jax.random.fold_in(streams_of[6], 71), 0),
        "w_keyval": gaussian(streams_of[4], (SECTIONS, D, 2 * KVW), D ** -0.5, 0.125, ((0, 32), (1, 16))),
        "w_out": gaussian(streams_of[5], (SECTIONS, QW, D), QW ** -0.5, 0.1875, ((0, 32), (1, 16))),
    }


def norm_scale(values, gain):
    mean_square = lax.optimization_barrier(jnp.mean(values * values, axis=-1, keepdims=True))
    return values * lax.rsqrt(mean_square + 1e-06) * gain

def rotary(heads_in, positions):
    half = heads_in.shape[-1] // 2
    freq = 10000.0 ** (-(jnp.arange(half, dtype=jnp.float32) * 2.0) / heads_in.shape[-1])
    angle = positions[:, None] * freq[None, :]
    cosine = jnp.cos(angle)[:, None, :]
    sine = jnp.sin(angle)[:, None, :]
    first = heads_in[..., :half]
    second = heads_in[..., half:]
    return jnp.concatenate([first * cosine - second * sine, second * cosine + first * sine], axis=-1)

def attend(query, keys, values):
    length = query.shape[0]
    group = HEADS // KV_HEADS
    grouped = query.reshape(length, KV_HEADS, group, HEAD_DIM).astype(jnp.float32)
    scores = jnp.einsum('skgd,tkd->kgst', grouped, keys.astype(jnp.float32))
    capped = 50.0 * jnp.tanh(scores / 50.0)
    causal = jnp.arange(length)[:, None] >= jnp.arange(length)[None, :]
    weights = jnp.where(causal, jnp.exp(capped), 0.0)
    total = lax.optimization_barrier(jnp.sum(weights, axis=-1, keepdims=True))
    probs = (weights / total).astype(jnp.bfloat16)
    context = jnp.einsum('kgst,tkd->skgd', probs.astype(jnp.float32), values.astype(jnp.float32))
    return context.reshape(length, HEADS * HEAD_DIM).astype(jnp.bfloat16)

def section_layer(operands):
    incoming, pre, post, w_query, w_keyval, w_out = operands
    widened = incoming.astype(jnp.float32)
    normed = norm_scale(widened, pre).astype(jnp.bfloat16)
    qraw = jnp.dot(normed, w_query, preferred_element_type=jnp.float32)
    kvraw = jnp.dot(normed, w_keyval, preferred_element_type=jnp.float32)
    kv_cols = KV_HEADS * HEAD_DIM
    positions = jnp.arange(SEQ, dtype=jnp.float32)
    sequences = qraw.shape[0] // SEQ

    def one_sequence(index):
        rows_q = lax.dynamic_slice_in_dim(qraw, index * SEQ, SEQ, 0)
        rows_kv = lax.dynamic_slice_in_dim(kvraw, index * SEQ, SEQ, 0)
        query = (rotary(rows_q.reshape(SEQ, HEADS, HEAD_DIM), positions) * 144.0 ** (-0.5)).astype(jnp.bfloat16)
        keys = rotary(rows_kv[:, :kv_cols].reshape(SEQ, KV_HEADS, HEAD_DIM), positions).astype(jnp.bfloat16)
        values = rows_kv[:, kv_cols:].reshape(SEQ, KV_HEADS, HEAD_DIM).astype(jnp.bfloat16)
        return attend(query, keys, values)
    context = lax.map(one_sequence, jnp.arange(sequences, dtype=jnp.int32))
    context = context.reshape(sequences * SEQ, HEADS * HEAD_DIM)
    attended = jnp.dot(context, w_out, preferred_element_type=jnp.float32)
    return (widened + norm_scale(attended, post)).astype(jnp.bfloat16)

def reference(activations, pre_gain, post_gain, w_query, w_keyval, w_out):
    incoming = jnp.roll(activations, 1, axis=0)
    return lax.map(section_layer, (incoming, pre_gain, post_gain, w_query, w_keyval, w_out))
```

```python
import jax
import jax.numpy as jnp
from jax import lax
from jax.experimental import pallas as pl
from jax.experimental.pallas import tpu as pltpu
from jax.sharding import PartitionSpec as P

HEAD_DIM = 64
LANES = 128
BLOCK = 128
AXES = ("section", "fsdp")


def moved(value, section_step, flip):
    sections, width = lax.axis_size("section"), lax.axis_size("fsdp")
    pairs = [
        (s * width + f, ((s + section_step) % sections) * width + (f ^ flip))
        for s in range(sections)
        for f in range(width)
    ]
    return lax.ppermute(value, AXES, pairs)


def norm_scale(values, gain):
    mean_square = jnp.mean(values * values, axis=-1, keepdims=True)
    return values * lax.rsqrt(mean_square + 1e-06) * gain


def rotary_tables(length):
    half = HEAD_DIM // 2
    positions = jnp.arange(length, dtype=jnp.float32)
    freq = 10000.0 ** (-(jnp.arange(half, dtype=jnp.float32) * 2.0) / HEAD_DIM)
    angle = positions[:, None] * freq[None, :]
    cosine, sine = jnp.cos(angle), jnp.sin(angle)
    return (
        jnp.concatenate([cosine] * 4, axis=1),
        jnp.concatenate([-sine, sine, -sine, sine], axis=1),
    )


def attention_kernel(raw_ref, cosine_ref, sine_ref, context_ref):
    length = raw_ref.shape[0]
    q_tiles = 2 * context_ref.shape[2] // LANES
    kv_tiles = q_tiles // 2
    lane = lax.broadcasted_iota(jnp.int32, (1, LANES), 1)
    in_first = lane % HEAD_DIM < HEAD_DIM // 2
    low = lane < HEAD_DIM
    cosine, sine = cosine_ref[...], sine_ref[...]

    def tile(index):
        return raw_ref[:, index * LANES : (index + 1) * LANES]

    def rotated(values):
        swapped = jnp.where(
            in_first,
            pltpu.roll(values, LANES - HEAD_DIM // 2, 1),
            pltpu.roll(values, HEAD_DIM // 2, 1),
        )
        return values * cosine + swapped * sine

    def twice(values):
        other = pltpu.roll(values, HEAD_DIM, 1)
        return (
            jnp.where(low, values, other).astype(jnp.bfloat16),
            jnp.where(low, other, values).astype(jnp.bfloat16),
        )

    below = lax.broadcasted_iota(jnp.int32, (BLOCK, BLOCK), 0) >= lax.broadcasted_iota(
        jnp.int32, (BLOCK, BLOCK), 1
    )
    for pair in range(kv_tiles):
        keys = twice(rotated(tile(q_tiles + pair)))
        values = twice(tile(q_tiles + kv_tiles + pair))
        tiles = {}
        for member in range(2):
            at = 2 * pair + member
            query = rotated(tile(at)) * 144.0 ** (-0.5)
            query_low = jnp.where(low, query, 0.0).astype(jnp.bfloat16)
            query_high = jnp.where(low, 0.0, query).astype(jnp.bfloat16)
            for start in range(0, length, BLOCK):
                stop = start + BLOCK
                parts = []
                for part in (query_low, query_high):
                    scores = lax.dot_general(
                        part[start:stop],
                        keys[member][:stop],
                        (((1,), (1,)), ((), ())),
                        preferred_element_type=jnp.float32,
                    )
                    weights = jnp.exp(50.0 * jnp.tanh(scores / 50.0))
                    edge = jnp.where(below, weights[:, start:], 0.0)
                    if start:
                        weights = jnp.concatenate([weights[:, :start], edge], axis=1)
                    else:
                        weights = edge
                    total = jnp.sum(weights, axis=-1, keepdims=True)
                    probs = (weights / total).astype(jnp.bfloat16)
                    parts.append(
                        jnp.dot(probs, values[member][:stop], preferred_element_type=jnp.float32)
                    )
                tiles[member, start] = parts
        for start in range(0, length, BLOCK):
            for parity in range(2):
                context_ref[
                    parity, start : start + BLOCK, pair * LANES : (pair + 1) * LANES
                ] = jnp.where(
                    low, tiles[0, start][parity], tiles[1, start][parity]
                ).astype(jnp.bfloat16)


def half_context(incoming, gain, weights, tables):
    length = incoming.shape[0]
    normed = norm_scale(incoming.astype(jnp.float32), gain).astype(jnp.bfloat16)
    raw = jnp.dot(normed, weights, preferred_element_type=jnp.float32)
    heads_width = weights.shape[1] // 2
    return pl.pallas_call(
        attention_kernel,
        out_shape=jax.ShapeDtypeStruct((2, length, heads_width // 2), jnp.bfloat16),
        compiler_params=pltpu.CompilerParams(vmem_limit_bytes=40 * 1024 * 1024),
        cost_estimate=pl.CostEstimate(
            flops=4 * length * length * heads_width,
            bytes_accessed=length * heads_width * 10,
            transcendentals=2 * length * length * heads_width // HEAD_DIM,
        ),
    )(raw, *tables)


def after(value, *others):
    return lax.optimization_barrier((value, *others))[0]


def body(activations, pre_gain, post_gain, w_query, w_keyval, w_out):
    width = lax.axis_size("fsdp")
    core = lax.axis_index("fsdp") % 2
    core_groups = [list(range(c, width, 2)) for c in range(2)]

    def gather_core(value):
        return lax.all_gather(value, "fsdp", axis=0, axis_index_groups=core_groups)

    incoming = moved(activations[0], 1, 0)
    gathered = gather_core(jnp.concatenate([w_query[0], w_keyval[0]], axis=1))
    out_mine = gather_core(w_out[0])
    gathered, incoming = lax.optimization_barrier((gathered, incoming))
    other = moved(gathered, 0, 1)
    even = jnp.where(core == 0, gathered, other)
    odd = jnp.where(core == 0, other, gathered)
    weights = jnp.stack([even, odd], axis=1).reshape(-1, gathered.shape[-1])
    tables = rotary_tables(incoming.shape[0])
    context = half_context(incoming, pre_gain[0], weights, tables)
    out_mine = after(out_mine, context)
    out_theirs = moved(out_mine, 0, 1)
    attended = jnp.dot(
        jnp.where(core == 0, context[0], context[1]),
        out_mine.reshape(-1, out_mine.shape[-1]),
        preferred_element_type=jnp.float32,
    ) + jnp.dot(
        jnp.where(core == 0, context[1], context[0]),
        out_theirs.reshape(-1, out_theirs.shape[-1]),
        preferred_element_type=jnp.float32,
    )
    advanced = incoming.astype(jnp.float32) + norm_scale(attended, post_gain[0])
    return advanced.astype(jnp.bfloat16)[None]


def solution(mesh):
    in_specs = (
        P("section", "fsdp", None),
        P("section", None),
        P("section", None),
        P("section", "fsdp", None),
        P("section", "fsdp", None),
        P("section", "fsdp", None),
    )
    out_specs = P("section", "fsdp", None)
    return jax.shard_map(body, mesh=mesh, in_specs=in_specs, out_specs=out_specs, check_vma=False)
```

```python
import functools

import jax
import jax.numpy as jnp
from jax import lax
from jax.experimental import pallas as pl
from jax.experimental.pallas import tpu as pltpu
from jax.sharding import PartitionSpec as P

HEAD_DIM = 64
LANES = 128
BLOCK = 128
CAP = 50.0
AXES = ("section", "fsdp")


def moved(value, section_step, flip):
    sections, width = lax.axis_size("section"), lax.axis_size("fsdp")
    pairs = [
        (s * width + f, ((s + section_step) % sections) * width + (f ^ flip))
        for s in range(sections)
        for f in range(width)
    ]
    return lax.ppermute(value, AXES, pairs)


def norm_scale(values, gain):
    mean_square = jnp.mean(values * values, axis=-1, keepdims=True)
    return values * lax.rsqrt(mean_square + 1e-06) * gain


def rotary_tables(length):
    half = HEAD_DIM // 2
    positions = jnp.arange(length, dtype=jnp.float32)
    freq = 10000.0 ** (-(jnp.arange(half, dtype=jnp.float32) * 2.0) / HEAD_DIM)
    angle = positions[:, None] * freq[None, :]
    cosine, sine = jnp.cos(angle), jnp.sin(angle)
    return (
        jnp.concatenate([cosine] * 4, axis=1),
        jnp.concatenate([-sine, sine, -sine, sine], axis=1),
    )


def packed(rows, columns):
    count, width = rows.shape
    side = columns // width
    rest = columns - side * width
    deep = count * width // columns
    pieces = [(deep, i * deep, 0, 0, i * width, width) for i in range(side)]
    last = count - side * deep
    pieces += [
        (last, side * deep, at * rest, at * last, side * width, rest)
        for at in range(width // rest)
    ]
    laid = [rows[r : r + n, c : c + m] for n, r, c, _, _, m in pieces]
    tail = jnp.concatenate(laid[side:], axis=0)
    return jnp.concatenate(laid[:side] + [tail], axis=1), pieces


def attention(raw, cosine_ref, sine_ref, store):
    length, width = raw.shape
    q_tiles = width // 2 // LANES
    kv_tiles = q_tiles // 2
    lane = lax.broadcasted_iota(jnp.int32, (1, LANES), 1)
    in_first = lane % HEAD_DIM < HEAD_DIM // 2
    low = lane < HEAD_DIM
    below = lax.broadcasted_iota(jnp.int32, (BLOCK, BLOCK), 0) >= lax.broadcasted_iota(
        jnp.int32, (BLOCK, BLOCK), 1
    )
    below = jnp.concatenate([below, below], axis=0)

    def tile(index):
        return raw[:, index * LANES : (index + 1) * LANES]

    def rotated(values):
        swapped = jnp.where(
            in_first,
            pltpu.roll(values, LANES - HEAD_DIM // 2, 1),
            pltpu.roll(values, HEAD_DIM // 2, 1),
        )
        return values * cosine_ref[...] + swapped * sine_ref[...]

    def twice(values):
        other = pltpu.roll(values, HEAD_DIM, 1)
        return (
            jnp.where(low, values, other).astype(jnp.bfloat16),
            jnp.where(low, other, values).astype(jnp.bfloat16),
        )

    for pair in range(kv_tiles):
        keys = twice(rotated(tile(q_tiles + pair)))
        values = twice(tile(q_tiles + kv_tiles + pair))
        tiles = {}
        for member in range(2):
            query = rotated(tile(2 * pair + member)) * 144.0 ** (-0.5)
            query_low = jnp.where(low, query, 0.0).astype(jnp.bfloat16)
            query_high = jnp.where(low, 0.0, query).astype(jnp.bfloat16)
            for start in range(0, length, BLOCK):
                stop = start + BLOCK
                both = jnp.concatenate([query_low[start:stop], query_high[start:stop]], axis=0)
                scores = lax.dot_general(
                    both,
                    keys[member][:stop],
                    (((1,), (1,)), ((), ())),
                    preferred_element_type=jnp.float32,
                )
                weight = jnp.exp(CAP * jnp.tanh(scores * (1.0 / CAP)))
                edge = jnp.where(below, weight[:, start:], 0.0)
                weight = jnp.concatenate([weight[:, :start], edge], axis=1) if start else edge
                total = jnp.sum(weight, axis=-1, keepdims=True)
                probs = (weight * (1.0 / total)).astype(jnp.bfloat16)
                tiles[member, start] = jnp.dot(
                    probs, values[member][:stop], preferred_element_type=jnp.float32
                )
        for start in range(0, length, BLOCK):
            for parity in range(2):
                part = slice(parity * BLOCK, (parity + 1) * BLOCK)
                store(
                    parity, start, pair, jnp.where(low, tiles[0, start][part], tiles[1, start][part])
                )


def storing(context_ref):
    def store(parity, start, tile, result):
        context_ref[parity, start : start + BLOCK, tile * LANES : (tile + 1) * LANES] = (
            result.astype(jnp.bfloat16)
        )

    return store


def project_kernel(
    pieces, normed_ref, gathered_ref, cosine_ref, sine_ref, context_ref, raw_ref, weights, sems
):
    chips = gathered_ref.shape[0]
    depth = weights.shape[0] // chips
    copies = []
    for chip in range(chips):
        for at, (n, r, c, pr, pc, m) in enumerate(pieces):
            copy = pltpu.make_async_copy(
                gathered_ref.at[chip, pr : pr + n, pc : pc + m],
                weights.at[chip * depth + r : chip * depth + r + n, c : c + m],
                sems.at[chip, at],
            )
            copy.start()
            copies.append(copy)
    length = raw_ref.shape[0]
    half = weights.shape[0] // 2
    split = len(copies) // 2
    for copy in copies[:split]:
        copy.wait()
    raw = jnp.dot(
        normed_ref[length:, :half], weights[:half], preferred_element_type=jnp.float32
    )
    for copy in copies[split:]:
        copy.wait()
    raw += jnp.dot(normed_ref[length:, half:], weights[half:], preferred_element_type=jnp.float32)
    attention(raw, cosine_ref, sine_ref, storing(context_ref))
    raw_ref[...] = jnp.dot(normed_ref[:length, :], weights[...], preferred_element_type=jnp.float32)


def attend_kernel(raw_ref, cosine_ref, sine_ref, context_ref):
    attention(raw_ref[...], cosine_ref, sine_ref, storing(context_ref))


def finish_kernel(
    here_ref, there_ref, mine_ref, theirs_ref, incoming_ref, gain_ref, advanced_ref
):
    core = lax.rem(lax.axis_index("fsdp"), 2)
    depth = here_ref.shape[2]
    own = pl.ds(pl.multiple_of(core * depth, depth), depth)
    got = pl.ds(pl.multiple_of((1 - core) * depth, depth), depth)
    for start in range(0, incoming_ref.shape[0], BLOCK):
        rows = slice(start, start + BLOCK)
        attended = jnp.zeros((BLOCK, incoming_ref.shape[1]), jnp.float32)
        for parity, weights in ((core, mine_ref), (1 - core, theirs_ref)):
            for context_ref, part in ((here_ref, own), (there_ref, got)):
                attended += jnp.dot(
                    context_ref[parity, rows], weights[part, :], preferred_element_type=jnp.float32
                )
        advanced_ref[rows, :] = (
            incoming_ref[rows, :].astype(jnp.float32) + norm_scale(attended, gain_ref[...])
        ).astype(jnp.bfloat16)


def take_kernel(first, gathered_ref, rows_ref, sems):
    chips, last, _ = gathered_ref.shape
    depth = last - first
    copies = [
        pltpu.make_async_copy(
            gathered_ref.at[chip, first:last], rows_ref.at[chip * depth : (chip + 1) * depth], sems.at[chip]
        )
        for chip in range(chips)
    ]
    for copy in copies:
        copy.start()
    for copy in copies:
        copy.wait()


VMEM = pl.BlockSpec(memory_space=pltpu.VMEM)
IN_PLACE = pl.BlockSpec(memory_space=pl.ANY)


def params(megabytes):
    return pltpu.CompilerParams(vmem_limit_bytes=megabytes * 1024 * 1024)


def attention_cost(length, width, depth):
    return pl.CostEstimate(
        flops=4 * length * width * depth + 2 * length * length * width,
        bytes_accessed=2 * (2 * length * depth + depth * width),
        transcendentals=length * length * width // HEAD_DIM,
    )


def body(activations, pre_gain, post_gain, w_query, w_keyval, w_out):
    width = lax.axis_size("fsdp")
    core = lax.axis_index("fsdp") % 2
    core_groups = [list(range(c, width, 2)) for c in range(2)]
    wq, wkv, wo = w_query[0], w_keyval[0], w_out[0]
    q_half, kv_half = wq.shape[1] // 2, wkv.shape[1] // 4

    def columns(side):
        return jnp.concatenate(
            [
                wq[:, side * q_half : (side + 1) * q_half],
                wkv[:, side * kv_half : (side + 1) * kv_half],
                wkv[:, (2 + side) * kv_half : (3 + side) * kv_half],
            ],
            axis=1,
        )

    incoming = moved(activations[0], 1, 0)
    first, second = columns(0), columns(1)
    mine = jnp.where(core == 0, first, second)
    got = moved(jnp.where(core == 0, second, first), 0, 1)
    shards = jnp.concatenate([jnp.where(core == 0, mine, got), jnp.where(core == 0, got, mine)], axis=0)
    shards_packed, pieces = packed(shards, wo.shape[1])
    deep = shards_packed.shape[0]
    gathered = lax.all_gather(
        jnp.concatenate([shards_packed, wo], axis=0), "fsdp", axis=0, axis_index_groups=core_groups
    )
    chips = width // 2
    gathered = gathered.reshape(chips, -1, wo.shape[1])

    normed = norm_scale(incoming.astype(jnp.float32), pre_gain[0]).astype(jnp.bfloat16)
    normed = jnp.concatenate([normed, moved(normed, 0, 1)], axis=0)
    tables = rotary_tables(incoming.shape[0])
    gathered, normed, tables = lax.optimization_barrier((gathered, normed, tables))

    out_mine = pl.pallas_call(
        functools.partial(take_kernel, deep),
        out_shape=jax.ShapeDtypeStruct((chips * wo.shape[0], wo.shape[1]), wo.dtype),
        in_specs=[IN_PLACE],
        out_specs=VMEM,
        scratch_shapes=[pltpu.SemaphoreType.DMA((chips,))],
    )(gathered)
    out_theirs = moved(out_mine, 0, 1)
    length, depth = incoming.shape
    half_width = shards.shape[1]
    context_shape = jax.ShapeDtypeStruct((2, length, half_width // 4), jnp.bfloat16)
    context_away, raw = pl.pallas_call(
        functools.partial(project_kernel, pieces),
        out_shape=(context_shape, jax.ShapeDtypeStruct((length, half_width), jnp.float32)),
        in_specs=[VMEM, IN_PLACE, VMEM, VMEM],
        out_specs=(VMEM, VMEM),
        scratch_shapes=[
            pltpu.VMEM((depth, half_width), jnp.bfloat16),
            pltpu.SemaphoreType.DMA((chips, len(pieces))),
        ],
        compiler_params=params(40),
        cost_estimate=attention_cost(length, half_width, depth),
    )(normed, gathered, *tables)
    there = moved(context_away, 0, 1)
    here = pl.pallas_call(
        attend_kernel,
        out_shape=context_shape,
        in_specs=[VMEM, VMEM, VMEM],
        out_specs=VMEM,
        compiler_params=params(24),
        cost_estimate=attention_cost(length, half_width, 0),
    )(raw, *tables)
    advanced = pl.pallas_call(
        finish_kernel,
        out_shape=jax.ShapeDtypeStruct(incoming.shape, incoming.dtype),
        in_specs=[VMEM] * 6,
        out_specs=VMEM,
        compiler_params=params(32),
        cost_estimate=pl.CostEstimate(
            flops=2 * incoming.size * width * wo.shape[0],
            bytes_accessed=4 * incoming.size + 4 * out_mine.size,
            transcendentals=0,
        ),
    )(here, there, out_mine, out_theirs, incoming, post_gain)
    return advanced[None]


def solution(mesh):
    in_specs = (
        P("section", "fsdp", None),
        P("section", None),
        P("section", None),
        P("section", "fsdp", None),
        P("section", "fsdp", None),
        P("section", "fsdp", None),
    )
    out_specs = P("section", "fsdp", None)
    return jax.shard_map(body, mesh=mesh, in_specs=in_specs, out_specs=out_specs, check_vma=False)
```

```python
import functools

import jax
import jax.numpy as jnp
from jax import lax
from jax.experimental import pallas as pl
from jax.experimental.pallas import tpu as pltpu
from jax.sharding import PartitionSpec as P

HEAD_DIM = 64
LANES = 128
BLOCK = 128
CAP = 50.0
AXES = ("section", "fsdp")


def moved(value, section_step, flip):
    sections, width = lax.axis_size("section"), lax.axis_size("fsdp")
    pairs = [
        (s * width + f, ((s + section_step) % sections) * width + (f ^ flip))
        for s in range(sections)
        for f in range(width)
    ]
    return lax.ppermute(value, AXES, pairs)


def norm_scale(values, gain):
    mean_square = jnp.mean(values * values, axis=-1, keepdims=True)
    return values * lax.rsqrt(mean_square + 1e-06) * gain


def rotary_tables(length):
    half = HEAD_DIM // 2
    positions = jnp.arange(length, dtype=jnp.float32)
    freq = 10000.0 ** (-(jnp.arange(half, dtype=jnp.float32) * 2.0) / HEAD_DIM)
    angle = positions[:, None] * freq[None, :]
    cosine, sine = jnp.cos(angle), jnp.sin(angle)
    return (
        jnp.concatenate([cosine] * 4, axis=1),
        jnp.concatenate([-sine, sine, -sine, sine], axis=1),
    )


def packed(rows, columns):
    count, width = rows.shape
    side = columns // width
    rest = columns - side * width
    deep = count * width // columns
    pieces = [(deep, i * deep, 0, 0, i * width, width) for i in range(side)]
    last = count - side * deep
    pieces += [
        (last, side * deep, at * rest, at * last, side * width, rest)
        for at in range(width // rest)
    ]
    laid = [rows[r : r + n, c : c + m] for n, r, c, _, _, m in pieces]
    tail = jnp.concatenate(laid[side:], axis=0)
    return jnp.concatenate(laid[:side] + [tail], axis=1), pieces


def attention(raw, cosine_ref, sine_ref, store):
    length, width = raw.shape
    q_tiles = width // 2 // LANES
    kv_tiles = q_tiles // 2
    lane = lax.broadcasted_iota(jnp.int32, (1, LANES), 1)
    in_first = lane % HEAD_DIM < HEAD_DIM // 2
    low = lane < HEAD_DIM
    below = lax.broadcasted_iota(jnp.int32, (BLOCK, BLOCK), 0) >= lax.broadcasted_iota(
        jnp.int32, (BLOCK, BLOCK), 1
    )
    below = jnp.concatenate([below, below], axis=0)

    def tile(index):
        return raw[:, index * LANES : (index + 1) * LANES]

    def rotated(values):
        swapped = jnp.where(
            in_first,
            pltpu.roll(values, LANES - HEAD_DIM // 2, 1),
            pltpu.roll(values, HEAD_DIM // 2, 1),
        )
        return values * cosine_ref[...] + swapped * sine_ref[...]

    def twice(values):
        other = pltpu.roll(values, HEAD_DIM, 1)
        return (
            jnp.where(low, values, other).astype(jnp.bfloat16),
            jnp.where(low, other, values).astype(jnp.bfloat16),
        )

    for pair in range(kv_tiles):
        keys = twice(rotated(tile(q_tiles + pair)))
        values = twice(tile(q_tiles + kv_tiles + pair))
        tiles = {}
        for member in range(2):
            query = rotated(tile(2 * pair + member)) * 144.0 ** (-0.5)
            query_low = jnp.where(low, query, 0.0).astype(jnp.bfloat16)
            query_high = jnp.where(low, 0.0, query).astype(jnp.bfloat16)
            for start in range(0, length, BLOCK):
                stop = start + BLOCK
                both = jnp.concatenate([query_low[start:stop], query_high[start:stop]], axis=0)
                scores = lax.dot_general(
                    both,
                    keys[member][:stop],
                    (((1,), (1,)), ((), ())),
                    preferred_element_type=jnp.float32,
                )
                weight = jnp.exp(CAP * jnp.tanh(scores * (1.0 / CAP)))
                edge = jnp.where(below, weight[:, start:], 0.0)
                weight = jnp.concatenate([weight[:, :start], edge], axis=1) if start else edge
                total = jnp.sum(weight, axis=-1, keepdims=True)
                probs = (weight * (1.0 / total)).astype(jnp.bfloat16)
                tiles[member, start] = jnp.dot(
                    probs, values[member][:stop], preferred_element_type=jnp.float32
                )
        for start in range(0, length, BLOCK):
            for parity in range(2):
                part = slice(parity * BLOCK, (parity + 1) * BLOCK)
                store(
                    parity, start, pair, jnp.where(low, tiles[0, start][part], tiles[1, start][part])
                )


def storing(context_ref):
    def store(parity, start, tile, result):
        context_ref[parity, start : start + BLOCK, tile * LANES : (tile + 1) * LANES] = (
            result.astype(jnp.bfloat16)
        )

    return store


def project_kernel(
    pieces, normed_ref, gathered_ref, cosine_ref, sine_ref, context_ref, raw_ref, weights, sems
):
    chips = gathered_ref.shape[0]
    depth = weights.shape[0] // chips
    copies = []
    for chip in range(chips):
        for at, (n, r, c, pr, pc, m) in enumerate(pieces):
            copy = pltpu.make_async_copy(
                gathered_ref.at[chip, pr : pr + n, pc : pc + m],
                weights.at[chip * depth + r : chip * depth + r + n, c : c + m],
                sems.at[chip, at],
            )
            copy.start()
            copies.append(copy)
    length = raw_ref.shape[0]
    half = weights.shape[0] // 2
    split = len(copies) // 2
    for copy in copies[:split]:
        copy.wait()
    raw = jnp.dot(
        normed_ref[length:, :half], weights[:half], preferred_element_type=jnp.float32
    )
    for copy in copies[split:]:
        copy.wait()
    raw += jnp.dot(normed_ref[length:, half:], weights[half:], preferred_element_type=jnp.float32)
    attention(raw, cosine_ref, sine_ref, storing(context_ref))
    raw_ref[...] = jnp.dot(normed_ref[:length, :], weights[...], preferred_element_type=jnp.float32)


def attend_kernel(raw_ref, cosine_ref, sine_ref, context_ref):
    attention(raw_ref[...], cosine_ref, sine_ref, storing(context_ref))


def finish_kernel(
    here_ref, there_ref, mine_ref, theirs_ref, incoming_ref, gain_ref, advanced_ref
):
    core = lax.rem(lax.axis_index("fsdp"), 2)
    depth = here_ref.shape[2]
    own = pl.ds(pl.multiple_of(core * depth, depth), depth)
    got = pl.ds(pl.multiple_of((1 - core) * depth, depth), depth)
    for start in range(0, incoming_ref.shape[0], BLOCK):
        rows = slice(start, start + BLOCK)
        attended = jnp.zeros((BLOCK, incoming_ref.shape[1]), jnp.float32)
        for parity, weights in ((core, mine_ref), (1 - core, theirs_ref)):
            for context_ref, part in ((here_ref, own), (there_ref, got)):
                attended += jnp.dot(
                    context_ref[parity, rows], weights[part, :], preferred_element_type=jnp.float32
                )
        advanced_ref[rows, :] = (
            incoming_ref[rows, :].astype(jnp.float32) + norm_scale(attended, gain_ref[...])
        ).astype(jnp.bfloat16)


def take_kernel(first, gathered_ref, rows_ref, sems):
    chips, last, _ = gathered_ref.shape
    depth = last - first
    copies = [
        pltpu.make_async_copy(
            gathered_ref.at[chip, first:last], rows_ref.at[chip * depth : (chip + 1) * depth], sems.at[chip]
        )
        for chip in range(chips)
    ]
    for copy in copies:
        copy.start()
    for copy in copies:
        copy.wait()


VMEM = pl.BlockSpec(memory_space=pltpu.VMEM)
IN_PLACE = pl.BlockSpec(memory_space=pl.ANY)


def params(megabytes):
    return pltpu.CompilerParams(vmem_limit_bytes=megabytes * 1024 * 1024)


def attention_cost(length, width, depth):
    return pl.CostEstimate(
        flops=4 * length * width * depth + 2 * length * length * width,
        bytes_accessed=2 * (2 * length * depth + depth * width),
        transcendentals=length * length * width // HEAD_DIM,
    )


def body(activations, pre_gain, post_gain, w_query, w_keyval, w_out):
    width = lax.axis_size("fsdp")
    core = lax.axis_index("fsdp") % 2
    core_groups = [list(range(c, width, 2)) for c in range(2)]
    wq, wkv, wo = w_query[0], w_keyval[0], w_out[0]
    q_half, kv_half = wq.shape[1] // 2, wkv.shape[1] // 4

    def columns(side):
        return jnp.concatenate(
            [
                wq[:, side * q_half : (side + 1) * q_half],
                wkv[:, side * kv_half : (side + 1) * kv_half],
                wkv[:, (2 + side) * kv_half : (3 + side) * kv_half],
            ],
            axis=1,
        )

    incoming = moved(activations[0], 1, 0)
    first, second = columns(0), columns(1)
    mine = jnp.where(core == 0, first, second)
    got = moved(jnp.where(core == 0, second, first), 0, 1)
    shards = jnp.concatenate([jnp.where(core == 0, mine, got), jnp.where(core == 0, got, mine)], axis=0)
    shards_packed, pieces = packed(shards, wo.shape[1])
    deep = shards_packed.shape[0]
    gathered = lax.all_gather(
        jnp.concatenate([shards_packed, wo], axis=0), "fsdp", axis=0, axis_index_groups=core_groups
    )
    chips = width // 2
    gathered = gathered.reshape(chips, -1, wo.shape[1])

    normed = norm_scale(incoming.astype(jnp.float32), pre_gain[0]).astype(jnp.bfloat16)
    normed = jnp.concatenate([normed, moved(normed, 0, 1)], axis=0)
    tables = rotary_tables(incoming.shape[0])
    gathered, normed, tables = lax.optimization_barrier((gathered, normed, tables))

    out_mine = pl.pallas_call(
        functools.partial(take_kernel, deep),
        out_shape=jax.ShapeDtypeStruct((chips * wo.shape[0], wo.shape[1]), wo.dtype),
        in_specs=[IN_PLACE],
        out_specs=VMEM,
        scratch_shapes=[pltpu.SemaphoreType.DMA((chips,))],
    )(gathered)
    out_theirs = moved(out_mine, 0, 1)
    length, depth = incoming.shape
    half_width = shards.shape[1]
    context_shape = jax.ShapeDtypeStruct((2, length, half_width // 4), jnp.bfloat16)
    context_away, raw = pl.pallas_call(
        functools.partial(project_kernel, pieces),
        out_shape=(context_shape, jax.ShapeDtypeStruct((length, half_width), jnp.float32)),
        in_specs=[VMEM, IN_PLACE, VMEM, VMEM],
        out_specs=(VMEM, VMEM),
        scratch_shapes=[
            pltpu.VMEM((depth, half_width), jnp.bfloat16),
            pltpu.SemaphoreType.DMA((chips, len(pieces))),
        ],
        compiler_params=params(48),
        cost_estimate=attention_cost(length, half_width, depth),
    )(normed, gathered, *tables)
    there = moved(context_away, 0, 1)
    here = pl.pallas_call(
        attend_kernel,
        out_shape=context_shape,
        in_specs=[VMEM, VMEM, VMEM],
        out_specs=VMEM,
        compiler_params=params(24),
        cost_estimate=attention_cost(length, half_width, 0),
    )(raw, *tables)
    advanced = pl.pallas_call(
        finish_kernel,
        out_shape=jax.ShapeDtypeStruct(incoming.shape, incoming.dtype),
        in_specs=[VMEM] * 6,
        out_specs=VMEM,
        compiler_params=params(32),
        cost_estimate=pl.CostEstimate(
            flops=2 * incoming.size * width * wo.shape[0],
            bytes_accessed=4 * incoming.size + 4 * out_mine.size,
            transcendentals=0,
        ),
    )(here, there, out_mine, out_theirs, incoming, post_gain)
    return advanced[None]


def solution(mesh):
    in_specs = (
        P("section", "fsdp", None),
        P("section", None),
        P("section", None),
        P("section", "fsdp", None),
        P("section", "fsdp", None),
        P("section", "fsdp", None),
    )
    out_specs = P("section", "fsdp", None)
    return jax.shard_map(body, mesh=mesh, in_specs=in_specs, out_specs=out_specs, check_vma=False)
```

```python
import functools

import jax
import jax.numpy as jnp
from jax import lax
from jax.experimental import pallas as pl
from jax.experimental.pallas import tpu as pltpu
from jax.sharding import PartitionSpec as P

HEAD_DIM = 64
LANES = 128
BLOCK = 128
CAP = 50.0
AXES = ("section", "fsdp")


def moved(value, section_step, flip):
    sections, width = lax.axis_size("section"), lax.axis_size("fsdp")
    pairs = [
        (s * width + f, ((s + section_step) % sections) * width + (f ^ flip))
        for s in range(sections)
        for f in range(width)
    ]
    return lax.ppermute(value, AXES, pairs)


def norm_scale(values, gain):
    mean_square = jnp.mean(values * values, axis=-1, keepdims=True)
    return values * lax.rsqrt(mean_square + 1e-06) * gain


def rotary_tables(length):
    half = HEAD_DIM // 2
    positions = jnp.arange(length, dtype=jnp.float32)
    freq = 10000.0 ** (-(jnp.arange(half, dtype=jnp.float32) * 2.0) / HEAD_DIM)
    angle = positions[:, None] * freq[None, :]
    cosine, sine = jnp.cos(angle), jnp.sin(angle)
    return (
        jnp.concatenate([cosine] * 4, axis=1),
        jnp.concatenate([-sine, sine, -sine, sine], axis=1),
    )


def packed(rows, columns):
    count, width = rows.shape
    side = columns // width
    rest = columns - side * width
    deep = count * width // columns
    pieces = [(deep, i * deep, 0, 0, i * width, width) for i in range(side)]
    last = count - side * deep
    pieces += [
        (last, side * deep, at * rest, at * last, side * width, rest)
        for at in range(width // rest)
    ]
    laid = [rows[r : r + n, c : c + m] for n, r, c, _, _, m in pieces]
    tail = jnp.concatenate(laid[side:], axis=0)
    return jnp.concatenate(laid[:side] + [tail], axis=1), pieces


def attention(raw, cosine_ref, sine_ref, store):
    length, width = raw.shape
    q_tiles = width // 2 // LANES
    kv_tiles = q_tiles // 2
    lane = lax.broadcasted_iota(jnp.int32, (1, LANES), 1)
    in_first = lane % HEAD_DIM < HEAD_DIM // 2
    low = lane < HEAD_DIM
    below = lax.broadcasted_iota(jnp.int32, (BLOCK, BLOCK), 0) >= lax.broadcasted_iota(
        jnp.int32, (BLOCK, BLOCK), 1
    )
    below = jnp.concatenate([below, below], axis=0)

    def tile(index):
        return raw[:, index * LANES : (index + 1) * LANES]

    def rotated(values):
        swapped = jnp.where(
            in_first,
            pltpu.roll(values, LANES - HEAD_DIM // 2, 1),
            pltpu.roll(values, HEAD_DIM // 2, 1),
        )
        return values * cosine_ref[...] + swapped * sine_ref[...]

    def twice(values):
        other = pltpu.roll(values, HEAD_DIM, 1)
        return (
            jnp.where(low, values, other).astype(jnp.bfloat16),
            jnp.where(low, other, values).astype(jnp.bfloat16),
        )

    for pair in range(kv_tiles):
        keys = twice(rotated(tile(q_tiles + pair)))
        values = twice(tile(q_tiles + kv_tiles + pair))
        tiles = {}
        for member in range(2):
            query = rotated(tile(2 * pair + member)) * 144.0 ** (-0.5)
            query_low = jnp.where(low, query, 0.0).astype(jnp.bfloat16)
            query_high = jnp.where(low, 0.0, query).astype(jnp.bfloat16)
            for start in range(0, length, BLOCK):
                stop = start + BLOCK
                both = jnp.concatenate([query_low[start:stop], query_high[start:stop]], axis=0)
                scores = lax.dot_general(
                    both,
                    keys[member][:stop],
                    (((1,), (1,)), ((), ())),
                    preferred_element_type=jnp.float32,
                )
                weight = jnp.exp(CAP * jnp.tanh(scores * (1.0 / CAP)))
                edge = jnp.where(below, weight[:, start:], 0.0)
                weight = jnp.concatenate([weight[:, :start], edge], axis=1) if start else edge
                total = jnp.sum(weight, axis=-1, keepdims=True)
                probs = (weight * (1.0 / total)).astype(jnp.bfloat16)
                tiles[member, start] = jnp.dot(
                    probs, values[member][:stop], preferred_element_type=jnp.float32
                )
        for start in range(0, length, BLOCK):
            for parity in range(2):
                part = slice(parity * BLOCK, (parity + 1) * BLOCK)
                store(
                    parity, start, pair, jnp.where(low, tiles[0, start][part], tiles[1, start][part])
                )


def storing(context_ref):
    def store(parity, start, tile, result):
        context_ref[parity, start : start + BLOCK, tile * LANES : (tile + 1) * LANES] = (
            result.astype(jnp.bfloat16)
        )

    return store


def project_kernel(
    pieces, normed_ref, gathered_ref, cosine_ref, sine_ref, context_ref, raw_ref, weights, sems
):
    chips = gathered_ref.shape[0]
    depth = weights.shape[0] // chips
    copies = []
    for chip in range(chips):
        for at, (n, r, c, pr, pc, m) in enumerate(pieces):
            copy = pltpu.make_async_copy(
                gathered_ref.at[chip, pr : pr + n, pc : pc + m],
                weights.at[chip * depth + r : chip * depth + r + n, c : c + m],
                sems.at[chip, at],
            )
            copy.start()
            copies.append(copy)
    length = raw_ref.shape[0]
    half = weights.shape[0] // 2
    split = len(copies) // 2
    for copy in copies[:split]:
        copy.wait()
    raw = jnp.dot(
        normed_ref[length:, :half], weights[:half], preferred_element_type=jnp.float32
    )
    raw_ref[...] = jnp.dot(
        normed_ref[:length, :half], weights[:half], preferred_element_type=jnp.float32
    )
    for copy in copies[split:]:
        copy.wait()
    raw += jnp.dot(normed_ref[length:, half:], weights[half:], preferred_element_type=jnp.float32)
    attention(raw, cosine_ref, sine_ref, storing(context_ref))
    raw_ref[...] += jnp.dot(
        normed_ref[:length, half:], weights[half:], preferred_element_type=jnp.float32
    )


def attend_kernel(raw_ref, cosine_ref, sine_ref, context_ref):
    attention(raw_ref[...], cosine_ref, sine_ref, storing(context_ref))


def finish_kernel(
    here_ref, there_ref, mine_ref, theirs_ref, incoming_ref, gain_ref, advanced_ref
):
    core = lax.rem(lax.axis_index("fsdp"), 2)
    depth = here_ref.shape[2]
    own = pl.ds(pl.multiple_of(core * depth, depth), depth)
    got = pl.ds(pl.multiple_of((1 - core) * depth, depth), depth)
    for start in range(0, incoming_ref.shape[0], BLOCK):
        rows = slice(start, start + BLOCK)
        attended = jnp.zeros((BLOCK, incoming_ref.shape[1]), jnp.float32)
        for parity, weights in ((core, mine_ref), (1 - core, theirs_ref)):
            for context_ref, part in ((here_ref, own), (there_ref, got)):
                attended += jnp.dot(
                    context_ref[parity, rows], weights[part, :], preferred_element_type=jnp.float32
                )
        advanced_ref[rows, :] = (
            incoming_ref[rows, :].astype(jnp.float32) + norm_scale(attended, gain_ref[...])
        ).astype(jnp.bfloat16)


def take_kernel(first, gathered_ref, rows_ref, sems):
    chips, last, _ = gathered_ref.shape
    depth = last - first
    copies = [
        pltpu.make_async_copy(
            gathered_ref.at[chip, first:last], rows_ref.at[chip * depth : (chip + 1) * depth], sems.at[chip]
        )
        for chip in range(chips)
    ]
    for copy in copies:
        copy.start()
    for copy in copies:
        copy.wait()


VMEM = pl.BlockSpec(memory_space=pltpu.VMEM)
IN_PLACE = pl.BlockSpec(memory_space=pl.ANY)


def params(megabytes):
    return pltpu.CompilerParams(vmem_limit_bytes=megabytes * 1024 * 1024)


def attention_cost(length, width, depth):
    return pl.CostEstimate(
        flops=4 * length * width * depth + 2 * length * length * width,
        bytes_accessed=2 * (2 * length * depth + depth * width),
        transcendentals=length * length * width // HEAD_DIM,
    )


def body(activations, pre_gain, post_gain, w_query, w_keyval, w_out):
    width = lax.axis_size("fsdp")
    core = lax.axis_index("fsdp") % 2
    core_groups = [list(range(c, width, 2)) for c in range(2)]
    wq, wkv, wo = w_query[0], w_keyval[0], w_out[0]
    q_half, kv_half = wq.shape[1] // 2, wkv.shape[1] // 4

    def columns(side):
        return jnp.concatenate(
            [
                wq[:, side * q_half : (side + 1) * q_half],
                wkv[:, side * kv_half : (side + 1) * kv_half],
                wkv[:, (2 + side) * kv_half : (3 + side) * kv_half],
            ],
            axis=1,
        )

    incoming = moved(activations[0], 1, 0)
    first, second = columns(0), columns(1)
    mine = jnp.where(core == 0, first, second)
    got = moved(jnp.where(core == 0, second, first), 0, 1)
    shards = jnp.concatenate([jnp.where(core == 0, mine, got), jnp.where(core == 0, got, mine)], axis=0)
    shards_packed, pieces = packed(shards, wo.shape[1])
    deep = shards_packed.shape[0]
    gathered = lax.all_gather(
        jnp.concatenate([shards_packed, wo], axis=0), "fsdp", axis=0, axis_index_groups=core_groups
    )
    chips = width // 2
    gathered = gathered.reshape(chips, -1, wo.shape[1])

    normed = norm_scale(incoming.astype(jnp.float32), pre_gain[0]).astype(jnp.bfloat16)
    normed = jnp.concatenate([normed, moved(normed, 0, 1)], axis=0)
    tables = rotary_tables(incoming.shape[0])
    gathered, normed, tables = lax.optimization_barrier((gathered, normed, tables))

    out_mine = pl.pallas_call(
        functools.partial(take_kernel, deep),
        out_shape=jax.ShapeDtypeStruct((chips * wo.shape[0], wo.shape[1]), wo.dtype),
        in_specs=[IN_PLACE],
        out_specs=VMEM,
        scratch_shapes=[pltpu.SemaphoreType.DMA((chips,))],
    )(gathered)
    out_theirs = moved(out_mine, 0, 1)
    length, depth = incoming.shape
    half_width = shards.shape[1]
    context_shape = jax.ShapeDtypeStruct((2, length, half_width // 4), jnp.bfloat16)
    context_away, raw = pl.pallas_call(
        functools.partial(project_kernel, pieces),
        out_shape=(context_shape, jax.ShapeDtypeStruct((length, half_width), jnp.float32)),
        in_specs=[VMEM, IN_PLACE, VMEM, VMEM],
        out_specs=(VMEM, VMEM),
        scratch_shapes=[
            pltpu.VMEM((depth, half_width), jnp.bfloat16),
            pltpu.SemaphoreType.DMA((chips, len(pieces))),
        ],
        compiler_params=params(48),
        cost_estimate=attention_cost(length, half_width, depth),
    )(normed, gathered, *tables)
    there = moved(context_away, 0, 1)
    here = pl.pallas_call(
        attend_kernel,
        out_shape=context_shape,
        in_specs=[VMEM, VMEM, VMEM],
        out_specs=VMEM,
        compiler_params=params(24),
        cost_estimate=attention_cost(length, half_width, 0),
    )(raw, *tables)
    advanced = pl.pallas_call(
        finish_kernel,
        out_shape=jax.ShapeDtypeStruct(incoming.shape, incoming.dtype),
        in_specs=[VMEM] * 6,
        out_specs=VMEM,
        compiler_params=params(32),
        cost_estimate=pl.CostEstimate(
            flops=2 * incoming.size * width * wo.shape[0],
            bytes_accessed=4 * incoming.size + 4 * out_mine.size,
            transcendentals=0,
        ),
    )(here, there, out_mine, out_theirs, incoming, post_gain)
    return advanced[None]


def solution(mesh):
    in_specs = (
        P("section", "fsdp", None),
        P("section", None),
        P("section", None),
        P("section", "fsdp", None),
        P("section", "fsdp", None),
        P("section", "fsdp", None),
    )
    out_specs = P("section", "fsdp", None)
    return jax.shard_map(body, mesh=mesh, in_specs=in_specs, out_specs=out_specs, check_vma=False)
```
